32 devices in a mesh: sx: 4 (over y, x), sy: 8 (over z, core).
Axes of the slice: x: 2, y: 2, z: 4, core: 2. Of those that a mesh axis runs over, the one named last changes fastest.
Arguments:
- interior_rhs: bfloat16 [4, 8, 2048, 1024], P('sx', 'sy'), may hold values from -6 to 6
- interface_coupling: bfloat16 [4, 8, 1024, 2048], P('sx', 'sy'), may hold values from -0.125 to 0.125
- interface_local: float32 [4, 8, 1024, 1024], P('sx', 'sy'), may hold values from -6 to 6
- off_blocks: bfloat16 [4, 8, 16, 4, 128, 128], P('sx', 'sy'), may hold values from -0.125 to 0.125
- diag_inverse: bfloat16 [4, 8, 16, 128, 128], P('sx', 'sy')
- block_pattern: int32 [4, 8, 16, 4], P('sx', 'sy'), may hold values from 0 to 15
- face_order: int32 [4, 8, 2, 512], P('sx', 'sy'), may hold values from 0 to 511, each once within a row
- krylov_map: int32 [4, 8, 1024], P('sx', 'sy'), may hold values from 0 to 1023, each once within a row
Outputs:
- krylov_rows: float32 [4, 8, 1024, 1024], P('sx', 'sy')
The draws below stay inside these ranges and needn't reach their ends.
Inputs may be any that keep to these rules, and one draw needn't show every extreme that they name: Each face_order[i, j, f] is a permutation of 0 to 511. Each krylov_map[i, j] is a permutation of 0 to 1023.
All inputs are finite; a program needn't handle non-finite values.
Results may differ from the reference program's by a relative error of at most 0.0037.
Values sent between devices are 32-bit elements; how exact they have to be, the bound alone decides.
A program may use at most 128 MiB of HBM per device.

```python
import jax
import jax.numpy as jnp
from jax import lax

BS = 128
FACE = 512
NB = 16
NNZ = 4
SWEEPS = 3
ROWS = 1024
NI = 2048
SHARE = 128
N_SX = 4
N_SY = 8


def draw_diag_inverse(key, part):
    shape = (N_SX, N_SY, NB, BS, BS)
    noise = jax.random.normal(key, shape, jnp.float32)
    eye = jnp.eye(BS, dtype=jnp.float32)
    return (eye + 0.3 * noise / jnp.sqrt(jnp.float32(BS))).astype(jnp.bfloat16)


def touch_ends(values, rng, least, largest):
    spot = [jax.random.randint(jax.random.fold_in(rng, axis), (), 0, length) for axis, length in enumerate(values.shape)]
    main_axis = values.shape.index(max(values.shape))
    next_to = spot[:main_axis] + [(spot[main_axis] + 1) % values.shape[main_axis]] + spot[main_axis + 1:]
    return values.at[tuple(spot)].set(least).at[tuple(next_to)].set(largest)


def level_of(key, shape, split, smallest, top_value):
    def one(dim, blocks):
        draws = jax.random.uniform(jax.random.fold_in(jax.random.fold_in(key, 6), dim), (blocks,), jnp.float32, smallest / len(split), top_value / len(split))
        return jnp.repeat(jnp.exp(draws), shape[dim] // blocks).reshape((-1,) + (1,) * (len(shape) - dim - 1))

    level = one(*split[0])
    for cut in split[1:]:
        level = level * one(*cut)
    return level


def gaussian(own_key, shape, scale, limit, pieces=(), kind=jnp.bfloat16):
    level = level_of(own_key, shape, pieces, -0.22, 0.18) if pieces else 1.0
    drawn = jax.random.normal(own_key, shape, jnp.float32) * scale * level
    return jnp.minimum(jnp.maximum(drawn, -limit), limit).astype(kind)


def setup_inputs(seed: int = 0) -> dict:
    seeds = jax.random.split(jax.random.key(seed), 9)
    return {
        "interior_rhs": gaussian(seeds[0], (N_SX, N_SY, NI, ROWS), 1.0, 6.0, ((0, 4), (1, 8))),
        "interface_coupling": gaussian(seeds[1], (N_SX, N_SY, ROWS, NI), NI ** -0.5, 0.125, ((0, 4), (1, 8))),
        "interface_local": gaussian(seeds[2], (N_SX, N_SY, ROWS, ROWS), 1.0, 6.0, ((0, 4), (1, 8)), jnp.float32),
        "off_blocks": gaussian(seeds[3], (N_SX, N_SY, NB, NNZ, BS, BS), (4 * NNZ * BS) ** -0.5, 0.125, ((0, 4), (1, 8))),
        "diag_inverse": draw_diag_inverse(jax.random.fold_in(seeds[8], 71), 0),
        "block_pattern": touch_ends(jax.random.randint(seeds[5], (N_SX, N_SY, NB, NNZ), 0, NB), jax.random.fold_in(seeds[5], 1), 0, NB - 1).astype(jnp.int32),
        "face_order": jax.vmap(lambda own: jax.random.permutation(own, FACE))(jax.random.split(seeds[6], N_SX * N_SY * 2)).reshape((N_SX, N_SY, 2, FACE)).astype(jnp.int32),
        "krylov_map": jax.vmap(lambda own: jax.random.permutation(own, ROWS))(jax.random.split(seeds[7], N_SX * N_SY)).reshape((N_SX, N_SY, ROWS)).astype(jnp.int32),
    }


def local_schur(rhs, coupling, own, offs, dinv, pattern):
    blocks = rhs.reshape(NB, BS, ROWS)
    dinv_f = dinv.astype(jnp.float32)
    offs_f = offs.astype(jnp.float32)
    z_now = jnp.einsum("bij,bjc->bic", dinv_f, blocks.astype(jnp.float32)).astype(jnp.bfloat16)
    for sweep in range(SWEEPS):
        nearby = z_now[pattern].astype(jnp.float32)
        acc = jnp.einsum("bkij,bkjc->bic", offs_f, nearby)
        resid = (blocks.astype(jnp.float32) - acc).astype(jnp.bfloat16)
        z_now = jnp.einsum("bij,bjc->bic", dinv_f, resid.astype(jnp.float32)).astype(jnp.bfloat16)
    return own - jnp.dot(coupling, z_now.reshape(NI, ROWS), preferred_element_type=jnp.float32)


def reference(interior_rhs, interface_coupling, interface_local, off_blocks, diag_inverse, block_pattern, face_order, krylov_map):
    count = N_SX * N_SY
    flat = (interior_rhs.reshape(count, NI, ROWS), interface_coupling.reshape(count, ROWS, NI),
            interface_local.reshape(count, ROWS, ROWS), off_blocks.reshape(count, NB, NNZ, BS, BS),
            diag_inverse.reshape(count, NB, BS, BS), block_pattern.reshape(count, NB, NNZ))
    schur = lax.map(lambda a: local_schur(*a), flat).reshape(N_SX, N_SY, ROWS, ROWS)
    ordr = face_order
    def shared_of(block, order):
        return block[order][:, order]
    def local_of(block, order):
        inverse = jnp.zeros((FACE,), jnp.int32).at[order].set(jnp.arange(FACE, dtype=jnp.int32))
        return block[inverse][:, inverse]
    face_a = schur[:, :, :FACE, :FACE]
    face_b = schur[:, :, FACE:, FACE:]
    shared_a = jax.vmap(jax.vmap(shared_of))(face_a, ordr[:, :, 0])
    shared_b = jax.vmap(jax.vmap(shared_of))(face_b, ordr[:, :, 1])
    partner_x = jnp.bitwise_xor(jnp.arange(N_SX, dtype=jnp.int32), 1)
    partner_y = jnp.bitwise_xor(jnp.arange(N_SY, dtype=jnp.int32), 1)
    got_a = shared_a[partner_x]
    got_b = shared_b[:, partner_y]
    new_a = face_a + jax.vmap(jax.vmap(local_of))(got_a, ordr[:, :, 0])
    new_b = face_b + jax.vmap(jax.vmap(local_of))(got_b, ordr[:, :, 1])
    top = jnp.concatenate([new_a, schur[:, :, :FACE, FACE:]], axis=3)
    bottom = jnp.concatenate([schur[:, :, FACE:, :FACE], new_b], axis=3)
    assembled = jnp.concatenate([top, bottom], axis=2)
    def place(tile, target):
        return jnp.zeros_like(tile).at[target].set(tile)
    placed = jax.vmap(jax.vmap(place))(assembled, krylov_map)
    placed = placed.reshape(N_SX, N_SY, N_SY, SHARE, ROWS)
    return jnp.transpose(placed, (0, 2, 1, 3, 4)).reshape(N_SX, N_SY, ROWS, ROWS)
```

```python
import functools

import jax
import jax.numpy as jnp
from jax import lax
from jax.experimental import pallas as pl
from jax.experimental.pallas import tpu as pltpu
from jax.sharding import PartitionSpec as P

SWEEPS = 3
GROUP = 4
F32 = jnp.float32
BF16 = jnp.bfloat16
VMEM_LIMIT = 50 * 2**20


def swapped(block, axis):
    count = lax.axis_size(axis)
    route = []
    for low in range(count):
        high = low | 1
        if high != low and high < count:
            route += [(low, high), (high, low)]
    return lax.ppermute(block, axis, route)


def dot(a, b):
    return jnp.dot(a, b, preferred_element_type=F32)


def halves(values):
    high = values.astype(BF16)
    return high, (values - high.astype(F32)).astype(BF16)


def picker_of(col, count):
    spot = lax.broadcasted_iota(jnp.int32, (col.shape[0], count), 1)
    return jnp.where(spot == col, F32(1), F32(0)).astype(BF16)


def picker_t_of(row, count, first=0):
    spot = lax.broadcasted_iota(jnp.int32, (count, row.shape[1]), 0) + first
    return jnp.where(spot == row, F32(1), F32(0)).astype(BF16)


def both_sides(left, block, right):
    high, low = halves(block)
    return dot(dot(left, high).astype(BF16), right) + dot(dot(left, low).astype(BF16), right)


def eliminate_kernel(
    side, pattern, rhs_hbm, offs_hbm, dinv_hbm, coupling_hbm, own_hbm, col_ref, row_ref,
    schur, shared, rhs, offs, dinv, coupling, own, z, sems,
):
    blocks, size, width = rhs.shape
    nnz = offs.shape[1]
    face = row_ref.shape[1]
    cols = pl.ds(side * width, width)
    moves = [
        pltpu.make_async_copy(dinv_hbm, dinv, sems.at[0]),
        pltpu.make_async_copy(rhs_hbm.at[:, :, cols], rhs, sems.at[1]),
        pltpu.make_async_copy(offs_hbm, offs, sems.at[2]),
        pltpu.make_async_copy(coupling_hbm, coupling, sems.at[3]),
        pltpu.make_async_copy(own_hbm.at[:, cols], own, sems.at[4]),
    ]
    for move in moves:
        move.start()
    moves[0].wait()
    moves[1].wait()

    @pl.loop(0, blocks // GROUP)
    def _(group):
        for part in range(GROUP):
            b = group * GROUP + part
            z[0, b] = dot(dinv[b], rhs[b]).astype(BF16)

    moves[2].wait()
    for sweep in range(SWEEPS):
        old, new = sweep % 2, (sweep + 1) % 2

        @pl.loop(0, blocks // GROUP)
        def _(group):
            for part in range(GROUP):
                b = group * GROUP + part
                row = jnp.concatenate([offs[b, k] for k in range(nnz)], axis=1)
                near = jnp.concatenate([z[old, pattern[b, k]] for k in range(nnz)], axis=0)
                resid = (rhs[b].astype(F32) - dot(row, near)).astype(BF16)
                z[new, b] = dot(dinv[b], resid).astype(BF16)

    moves[3].wait()
    moves[4].wait()
    rows = own.shape[0]
    tile = rows // 4

    @pl.loop(0, 4)
    def _(step):
        span = pl.ds(pl.multiple_of(step * tile, tile), tile)
        done = z[SWEEPS % 2].reshape(blocks * size, width)
        schur[span, :] = own[span, :] - dot(coupling[span, :], done)

    left = picker_of(col_ref[...], face)
    right = picker_t_of(row_ref[...], face)
    shared[...] = both_sides(left, schur[pl.ds(side * face, face), :], right)


def eliminate(side, pattern, rhs, offs, dinv, coupling, own, col, row):
    blocks, size, all_cols = rhs.shape
    face = row.shape[1]
    rows = own.shape[0]
    width = all_cols // 2
    macs = blocks * size * width * size * (1 + SWEEPS * (1 + offs.shape[1])) + rows * blocks * size * width
    anywhere = pl.BlockSpec(memory_space=pl.ANY)
    vmem = pl.BlockSpec(memory_space=pltpu.VMEM)
    return pl.pallas_call(
        functools.partial(eliminate_kernel, side),
        out_shape=(
            jax.ShapeDtypeStruct((rows, width), F32),
            jax.ShapeDtypeStruct((face, face), F32),
        ),
        in_specs=[pl.BlockSpec(memory_space=pltpu.SMEM)] + [anywhere] * 5 + [vmem] * 2,
        out_specs=(vmem, vmem),
        scratch_shapes=[
            pltpu.VMEM((blocks, size, width), BF16),
            pltpu.VMEM(offs.shape, BF16),
            pltpu.VMEM(dinv.shape, BF16),
            pltpu.VMEM(coupling.shape, BF16),
            pltpu.VMEM((rows, width), F32),
            pltpu.VMEM((2, blocks, size, width), BF16),
            pltpu.SemaphoreType.DMA((5,)),
        ],
        compiler_params=pltpu.CompilerParams(vmem_limit_bytes=VMEM_LIMIT),
        cost_estimate=pl.CostEstimate(flops=4 * macs, bytes_accessed=12 * 2**20, transcendentals=0),
    )(pattern, rhs, offs, dinv, coupling, own, col, row)


def place_kernel(side, schur, got, col_ref, row_ref, target_ref, placed, high, low):
    face = row_ref.shape[1]
    rows = schur.shape[0]
    mine = pl.ds(side * face, face)
    rest = pl.ds((1 - side) * face, face)
    high[rest, :], low[rest, :] = halves(schur[rest, :])
    back = both_sides(picker_t_of(row_ref[...], face), got[...], picker_of(col_ref[...], face))
    high[mine, :], low[mine, :] = halves(schur[mine, :] + back)
    tile = rows // 4

    @pl.loop(0, 4)
    def _(step):
        first = pl.multiple_of(step * tile, tile)
        placer = picker_t_of(target_ref[...], tile, first)
        placed[pl.ds(first, tile), :] = dot(placer, high[...]) + dot(placer, low[...])


def place(side, schur, got, col, row, target):
    rows, width = schur.shape
    vmem = pl.BlockSpec(memory_space=pltpu.VMEM)
    return pl.pallas_call(
        functools.partial(place_kernel, side),
        out_shape=jax.ShapeDtypeStruct((rows, width), F32),
        in_specs=[vmem] * 5,
        out_specs=vmem,
        scratch_shapes=[pltpu.VMEM((rows, width), BF16), pltpu.VMEM((rows, width), BF16)],
        compiler_params=pltpu.CompilerParams(vmem_limit_bytes=VMEM_LIMIT),
        cost_estimate=pl.CostEstimate(
            flops=4 * rows * rows * width, bytes_accessed=5 * 2**20, transcendentals=0
        ),
    )(schur, got, col, row, target)


def send(placed):
    return lax.all_to_all(placed, "sy", split_axis=0, concat_axis=0, tiled=True)


def local(
    interior_rhs,
    interface_coupling,
    interface_local,
    off_blocks,
    diag_inverse,
    block_pattern,
    face_order,
    krylov_map,
):
    coupling = interface_coupling[0, 0]
    own = interface_local[0, 0]
    offs = off_blocks[0, 0]
    dinv = diag_inverse[0, 0]
    pattern = block_pattern[0, 0]
    rhs = interior_rhs[0, 0].reshape(dinv.shape[0], dinv.shape[1], own.shape[1])
    orders = face_order[0, 0]
    target = krylov_map[0]
    col = [orders[f][:, None] for f in range(2)]
    row = [orders[f][None, :] for f in range(2)]

    schur_b, shared_b = eliminate(1, pattern, rhs, offs, dinv, coupling, own, col[1], row[1])
    got_b = swapped(shared_b, "sy")
    placed_b = place(1, schur_b, got_b, col[1], row[1], target)
    placed_b, pattern = lax.optimization_barrier((placed_b, pattern))
    moved_b = send(placed_b)
    schur_a, shared_a = eliminate(0, pattern, rhs, offs, dinv, coupling, own, col[0], row[0])
    got_a = swapped(shared_a, "sx")
    placed_a = place(0, schur_a, got_a, col[0], row[0], target)
    moved_a = send(placed_a)
    return jnp.concatenate([moved_a, moved_b], axis=1)[None, None]


def solution(mesh):
    return jax.shard_map(
        local,
        mesh=mesh,
        in_specs=(
            P("sx", "sy", None, None),
            P("sx", "sy", None, None),
            P("sx", "sy", None, None),
            P("sx", "sy", None, None, None, None),
            P("sx", "sy", None, None, None),
            P("sx", "sy", None, None),
            P("sx", "sy", None, None),
            P("sx", "sy", None),
        ),
        out_specs=P("sx", "sy", None, None),
        check_vma=False,
    )
```

```python
import functools

import jax
import jax.numpy as jnp
from jax import lax
from jax.experimental import pallas as pl
from jax.experimental.pallas import tpu as pltpu
from jax.sharding import PartitionSpec as P

SWEEPS = 3
GROUP = 16
PAIR = 4
TILES = 2
F32 = jnp.float32
BF16 = jnp.bfloat16
VMEM_LIMIT = 50 * 2**20
PLACE_LIMIT = 18 * 2**20


def swapped(block, axis):
    count = lax.axis_size(axis)
    route = []
    for low in range(count):
        high = low | 1
        if high != low and high < count:
            route += [(low, high), (high, low)]
    return lax.ppermute(block, axis, route)


def dot(a, b):
    return jnp.dot(a, b, preferred_element_type=F32)


def halves(values):
    high = values.astype(BF16)
    return high, (values - high.astype(F32)).astype(BF16)


def picker_of(col, count):
    spot = lax.broadcasted_iota(jnp.int32, (col.shape[0], count), 1)
    return jnp.where(spot == col, F32(1), F32(0)).astype(BF16)


def picker_t_of(row, count, first=0):
    spot = lax.broadcasted_iota(jnp.int32, (count, row.shape[1]), 0) + first
    return jnp.where(spot == row, F32(1), F32(0)).astype(BF16)


def both_sides(left, block, right):
    high, low = halves(block)
    return dot(dot(left, high).astype(BF16), right) + dot(dot(left, low).astype(BF16), right)


def eliminate_kernel(
    side, pattern, rhs_hbm, offs_hbm, dinv_hbm, coupling_hbm, own_hbm, col_ref, row_ref,
    schur, shared, rhs, offs, dinv, coupling, own, even, odd, sems,
):
    blocks, size, width = rhs.shape
    nnz = offs.shape[1]
    face = row_ref.shape[1]
    cols = pl.ds(side * width, width)
    moves = [
        pltpu.make_async_copy(dinv_hbm, dinv, sems.at[0]),
        pltpu.make_async_copy(rhs_hbm.at[:, :, cols], rhs, sems.at[1]),
        pltpu.make_async_copy(offs_hbm, offs, sems.at[2]),
        pltpu.make_async_copy(coupling_hbm, coupling, sems.at[3]),
        pltpu.make_async_copy(own_hbm.at[:, cols], own, sems.at[4]),
    ]
    for move in moves:
        move.start()
    moves[0].wait()
    moves[1].wait()

    @pl.loop(0, blocks // GROUP)
    def _(group):
        for part in range(GROUP):
            b = group * GROUP + part
            even[b] = dot(dinv[b], rhs[b]).astype(BF16)

    moves[2].wait()
    for sweep in range(SWEEPS):
        old, new = ((even, odd), (odd, even))[sweep % 2]

        @pl.loop(0, blocks // GROUP)
        def _(group):
            resid = []
            for part in range(GROUP):
                b = group * GROUP + part
                row = jnp.concatenate([offs[b, k] for k in range(nnz)], axis=1)
                near = jnp.concatenate([old[pattern[b, k]] for k in range(nnz)], axis=0)
                resid.append((rhs[b].astype(F32) - dot(row, near)).astype(BF16))
                if part % PAIR == PAIR - 1:
                    for late in range(part - PAIR + 1, part + 1):
                        spot = group * GROUP + late
                        new[spot] = dot(dinv[spot], resid[late]).astype(BF16)

    moves[3].wait()
    moves[4].wait()
    rows = own.shape[0]
    tile = rows // TILES
    last = (even, odd)[SWEEPS % 2]

    @pl.loop(0, TILES)
    def _(step):
        span = pl.ds(pl.multiple_of(step * tile, tile), tile)
        done = last[...].reshape(blocks * size, width)
        schur[span, :] = own[span, :] - dot(coupling[span, :], done)

    left = picker_of(col_ref[...], face)
    right = picker_t_of(row_ref[...], face)
    shared[...] = both_sides(left, schur[pl.ds(side * face, face), :], right)


def eliminate(side, pattern, rhs, offs, dinv, coupling, own, col, row):
    blocks, size, all_cols = rhs.shape
    face = row.shape[1]
    rows = own.shape[0]
    width = all_cols // 2
    macs = blocks * size * width * size * (1 + SWEEPS * (1 + offs.shape[1])) + rows * blocks * size * width
    anywhere = pl.BlockSpec(memory_space=pl.ANY)
    vmem = pl.BlockSpec(memory_space=pltpu.VMEM)
    return pl.pallas_call(
        functools.partial(eliminate_kernel, side),
        out_shape=(
            jax.ShapeDtypeStruct((rows, width), F32),
            jax.ShapeDtypeStruct((face, face), F32),
        ),
        in_specs=[pl.BlockSpec(memory_space=pltpu.SMEM)] + [anywhere] * 5 + [vmem] * 2,
        out_specs=(vmem, vmem),
        scratch_shapes=[
            pltpu.VMEM((blocks, size, width), BF16),
            pltpu.VMEM(offs.shape, BF16),
            pltpu.VMEM(dinv.shape, BF16),
            pltpu.VMEM(coupling.shape, BF16),
            pltpu.VMEM((rows, width), F32),
            pltpu.VMEM((blocks, size, width), BF16),
            pltpu.VMEM((blocks, size, width), BF16),
            pltpu.SemaphoreType.DMA((5,)),
        ],
        compiler_params=pltpu.CompilerParams(vmem_limit_bytes=VMEM_LIMIT),
        cost_estimate=pl.CostEstimate(flops=4 * macs, bytes_accessed=12 * 2**20, transcendentals=0),
    )(pattern, rhs, offs, dinv, coupling, own, col, row)


def place_kernel(side, schur, got, col_ref, row_ref, target_ref, placed, high, low):
    face = row_ref.shape[1]
    rows = schur.shape[0]
    mine = pl.ds(side * face, face)
    rest = pl.ds((1 - side) * face, face)
    high[rest, :], low[rest, :] = halves(schur[rest, :])
    back = both_sides(picker_t_of(row_ref[...], face), got[...], picker_of(col_ref[...], face))
    high[mine, :], low[mine, :] = halves(schur[mine, :] + back)
    tile = rows // 4

    @pl.loop(0, 4)
    def _(step):
        first = pl.multiple_of(step * tile, tile)
        placer = picker_t_of(target_ref[...], tile, first)
        placed[pl.ds(first, tile), :] = dot(placer, high[...]) + dot(placer, low[...])


def place(side, schur, got, col, row, target):
    rows, width = schur.shape
    vmem = pl.BlockSpec(memory_space=pltpu.VMEM)
    return pl.pallas_call(
        functools.partial(place_kernel, side),
        out_shape=jax.ShapeDtypeStruct((rows, width), F32),
        in_specs=[vmem] * 5,
        out_specs=vmem,
        scratch_shapes=[pltpu.VMEM((rows, width), BF16), pltpu.VMEM((rows, width), BF16)],
        compiler_params=pltpu.CompilerParams(vmem_limit_bytes=PLACE_LIMIT),
        cost_estimate=pl.CostEstimate(
            flops=4 * rows * rows * width, bytes_accessed=5 * 2**20, transcendentals=0
        ),
    )(schur, got, col, row, target)


def send(placed):
    return lax.all_to_all(placed, "sy", split_axis=0, concat_axis=0, tiled=True)


def local(
    interior_rhs,
    interface_coupling,
    interface_local,
    off_blocks,
    diag_inverse,
    block_pattern,
    face_order,
    krylov_map,
):
    coupling = interface_coupling[0, 0]
    own = interface_local[0, 0]
    offs = off_blocks[0, 0]
    dinv = diag_inverse[0, 0]
    pattern = block_pattern[0, 0]
    rhs = interior_rhs[0, 0].reshape(dinv.shape[0], dinv.shape[1], own.shape[1])
    orders = face_order[0, 0]
    target = krylov_map[0]
    col = [orders[f][:, None] for f in range(2)]
    row = [orders[f][None, :] for f in range(2)]

    schur_b, shared_b = eliminate(1, pattern, rhs, offs, dinv, coupling, own, col[1], row[1])
    got_b = swapped(shared_b, "sy")
    placed_b = place(1, schur_b, got_b, col[1], row[1], target)
    placed_b, pattern = lax.optimization_barrier((placed_b, pattern))
    moved_b = send(placed_b)
    schur_a, shared_a = eliminate(0, pattern, rhs, offs, dinv, coupling, own, col[0], row[0])
    got_a = swapped(shared_a, "sx")
    placed_a = place(0, schur_a, got_a, col[0], row[0], target)
    moved_a = send(placed_a)
    return jnp.concatenate([moved_a, moved_b], axis=1)[None, None]


def solution(mesh):
    return jax.shard_map(
        local,
        mesh=mesh,
        in_specs=(
            P("sx", "sy", None, None),
            P("sx", "sy", None, None),
            P("sx", "sy", None, None),
            P("sx", "sy", None, None, None, None),
            P("sx", "sy", None, None, None),
            P("sx", "sy", None, None),
            P("sx", "sy", None, None),
            P("sx", "sy", None),
        ),
        out_specs=P("sx", "sy", None, None),
        check_vma=False,
    )
```
